1024 devices in a mesh: dp: 64 (over x, z), expert: 16 (over y, core).
Axes of the slice: x: 8, y: 8, z: 8, core: 2. Of those that a mesh axis runs over, the one named last changes fastest.
Arguments:
- d_out: bfloat16 [131072, 5120], P(('dp', 'expert')), may hold values from -6 to 6
- routes: int32 [131072, 1], P(('dp', 'expert')), may hold values from 0 to 15; in each aligned block of 128 rows (0 to 127, 128 to 255, ...) at most 10 rows name the same one
- gates: bfloat16 [131072, 1], P(('dp', 'expert')), may hold values from 0.01 to 1, as said below
- slot_hidden: bfloat16 [64, 16, 16, 10, 768], P('dp', None, 'expert'), may hold values from -0.59765625 to 0.59765625
- w_down: bfloat16 [16, 768, 5120], P('expert'), may hold values from -0.078125 to 0.078125
- balance_coef: float32 [], replicated, may hold values from 0.5 to 2
Outputs:
- d_probs: float32 [131072, 16], P(('dp', 'expert'))
- d_hidden: bfloat16 [64, 16, 16, 10, 768], P('dp', None, 'expert')
The draws below stay inside these ranges and needn't reach their ends.
Inputs may be any that keep to these rules, and one draw needn't show every extreme that they name: `routes`: within each aligned block of 128 rows (the rows of one device) no expert is named by more than 10 pairs, a bound that some block reaches. `gates`: positive gate weights.
All inputs are finite; a program needn't handle non-finite values.
Results may differ from the reference program's by a relative error of at most 0.007.
Values may be sent and summed in bfloat16 or wider, within the bound.
No kernel may reach another device: no remote copies, remote signals or barrier semaphores. Data moves between devices by JAX's collectives and lax.ppermute only.
A program may use at most 64 MiB of HBM per device.

```python
import math
import jax
import jax.numpy as jnp
import numpy as np
from jax import lax

D = 5120
FFW = 768
TOP = 1
TOK_DEV = 128
EXPERTS = 16
CAP = 10
TOKENS = 131072
N_DP = 64
N_EXPERT = 16


def draw_gates(key, part):
    key = jax.random.fold_in(key, 7)
    position = (jnp.arange(TOKENS, dtype=jnp.float32) / TOKENS)[:, None]
    base = jax.random.uniform(key, (TOKENS, TOP), jnp.float32, 0.1, 1.0)
    ramp = 0.3 + 0.7 * position
    return (base * ramp).astype(jnp.bfloat16)


def steps_of(stream_key, extent, cuts, smallest, top_value):
    level, own = 1.0, jax.random.fold_in(stream_key, 6)
    for dim, parts in cuts:
        heights = jnp.exp(jax.random.uniform(jax.random.fold_in(own, dim), (parts,), jnp.float32, smallest / len(cuts), top_value / len(cuts)))
        level = level * jnp.repeat(heights, extent[dim] // parts).reshape([-1 if axis == dim else 1 for axis in range(len(extent))])
    return level


def shared_out(rng, own, number, rows, amount, top, limit, slope):
    ranking = jax.random.permutation(rng, amount)
    packed, common = shares(amount, rows * top, limit, slope, True), shares(amount, rows * top, limit, slope, False)
    places = jnp.arange(amount)

    def named(tallies, offset_by):
        used = int((tallies > 0).sum())
        fixed = max(1, used // 4)
        moved = fixed + (places - fixed + offset_by * (used - fixed)) % max(1, amount - fixed)
        return jnp.zeros((amount,), jnp.int32).at[ranking[jnp.where(places < fixed, places, moved)]].set(jnp.asarray(tallies, jnp.int32))

    tallies = jnp.where(number % 4 == 0, named(packed, number // 4), named(common, number - number // 4 - 1))
    mixed = jax.random.permutation(jax.random.fold_in(own, 3), amount)
    source_of, sink = mixed[0:amount // 2 * 2:2], mixed[1:amount // 2 * 2:2]
    room = jnp.minimum(tallies[source_of] - 1, limit - tallies[sink]) // 2
    room = jnp.where((source_of == ranking[0]) | (sink == ranking[0]) | (tallies[sink] == 0), 0, jnp.maximum(room, 0))
    moved = jax.random.randint(jax.random.fold_in(own, 4), (amount // 2,), 0, 1 << 20) % (room + 1)
    tallies = tallies.at[source_of].add(-moved).at[sink].add(moved)
    labels = jnp.searchsorted(jnp.cumsum(tallies), jnp.arange(rows * top), side="right").astype(jnp.int32)
    grid = labels.reshape(top, rows).T
    grid = grid[jax.random.permutation(jax.random.fold_in(own, 1), rows)]
    offset_by = jax.random.randint(jax.random.fold_in(own, 2), (rows, 1), 0, top)
    return jnp.take_along_axis(grid, (jnp.arange(top)[None, :] + offset_by) % top, axis=1)


def shares(count, total, most, skew, full):
    weights = [(1 << 20) // math.isqrt(grade ** skew) + 1 for grade in range(1, count + 1)]
    largest = most if full else min(most, max(-(-total // count), total * weights[0] // sum(weights)))
    least = 1 if total - largest >= count - 1 else 0
    counts, spare = [largest] + [least] * (count - 1), total - largest - least * (count - 1)
    while spare > 0:
        free = [i for i in range(1, count) if counts[i] < largest] or [i for i in range(1, count) if counts[i] < most]
        pool, left = sum([weights[i] for i in free]), spare
        for i in free:
            extra = min(most - counts[i], max(1, left * weights[i] // pool), spare)
            counts[i] = counts[i] + extra
            spare = spare - extra
    return np.array(counts)


def centred(rng, extent, scale, reach, split=(), held_as=jnp.bfloat16):
    entries = jax.random.normal(rng, extent, jnp.float32) * scale
    if len(split) > 0:
        entries = steps_of(rng, extent, split, -0.22, 0.18) * entries
    return jnp.clip(entries, min=-reach, max=reach).astype(held_as)


def setup_inputs(seed: int = 0) -> dict:
    streams_of = jax.random.split(jax.random.key(seed), 7)
    d_out = centred(streams_of[0], (TOKENS, D), 1.0, 6.0, ((0, 1024),))
    routes_keys = jax.random.split(jax.random.fold_in(streams_of[1], 1), TOKENS // TOK_DEV)
    routes_turns = jax.random.permutation(jax.random.fold_in(streams_of[1], 3), TOKENS // TOK_DEV)
    routes = jax.vmap(lambda own, number: shared_out(jax.random.fold_in(streams_of[1], 2), own, number, TOK_DEV, EXPERTS, TOP, CAP, 2))(routes_keys, routes_turns).reshape((TOKENS, TOP))
    gates = draw_gates(jax.random.fold_in(streams_of[6], 71), 0)
    slot_hidden = centred(streams_of[3], (N_DP, N_EXPERT, EXPERTS, CAP, FFW), 0.1, 0.59765625, ((0, 64), (2, 16)))
    w_down = centred(streams_of[4], (EXPERTS, FFW, D), D ** -0.5, 0.078125, ((0, 16),))
    balance_coef = jnp.clip(jax.random.uniform(streams_of[5], (), jnp.float32, 0.5, 2.0), 0.5, 2.0)
    return {"d_out": d_out, "routes": routes, "gates": gates, "slot_hidden": slot_hidden, "w_down": w_down, "balance_coef": balance_coef}


def reference(d_out, routes, gates, slot_hidden, w_down, balance_coef):
    blocks = TOKENS // TOK_DEV
    flat = routes.reshape(blocks, TOK_DEV * TOP).astype(jnp.int32)
    expert_ids = jnp.arange(EXPERTS, dtype=jnp.int32)
    onehot = (flat[:, :, None] == expert_ids[None, None, :]).astype(jnp.int32)
    ranks = jnp.sum((jnp.cumsum(onehot, 1) - onehot) * onehot, 2).astype(jnp.int32)
    block_idx = jnp.broadcast_to(jnp.arange(blocks, dtype=jnp.int32)[:, None], flat.shape)
    pair_idx = jnp.arange(TOK_DEV * TOP, dtype=jnp.int32)[None, :] // TOP
    token_idx = (block_idx * TOK_DEV + pair_idx).astype(jnp.int32)
    flat_gate = gates.reshape(blocks, TOK_DEV * TOP).astype(jnp.float32)
    slot_token = jnp.full((blocks, EXPERTS, CAP), -1, jnp.int32).at[block_idx, flat, ranks].set(token_idx)
    slot_gate = jnp.zeros((blocks, EXPERTS, CAP), jnp.float32).at[block_idx, flat, ranks].set(flat_gate)
    hidden = slot_hidden.reshape(blocks, EXPERTS, CAP, FFW)

    def one_expert(expert):
        toks = slot_token[:, expert]
        live = toks >= 0
        picked = d_out[jnp.maximum(toks, 0)]
        rows = jnp.where(live[:, :, None], picked, jnp.zeros_like(picked))
        weight = w_down[expert]
        y_out = jnp.dot(hidden[:, expert].reshape(-1, FFW), weight,
                        preferred_element_type=jnp.float32).astype(jnp.bfloat16).reshape(blocks, CAP, D)
        score = jnp.sum(rows.astype(jnp.float32) * y_out.astype(jnp.float32), -1)
        dproj = lax.dot_general(rows.reshape(-1, D), weight, (((1,), (1,)), ((), ())),
                                preferred_element_type=jnp.float32).reshape(blocks, CAP, FFW)
        grad = (dproj * slot_gate[:, expert][:, :, None]).astype(jnp.bfloat16)
        return score, grad

    scores, grads = lax.map(one_expert, expert_ids)
    d_hidden = jnp.transpose(grads, (1, 0, 2, 3)).reshape(N_DP, N_EXPERT, EXPERTS, CAP, FFW)
    pair_score = scores[flat, block_idx, ranks]
    mass = jnp.sum(onehot.astype(jnp.float32) * flat_gate[:, :, None], (0, 1))
    load = EXPERTS * mass / (TOP * TOKENS)
    routed = (onehot.astype(jnp.float32) * pair_score[:, :, None]).reshape(TOKENS, TOP, EXPERTS)
    d_probs = balance_coef * load[None, :] + jnp.sum(routed, 1)
    return d_probs, d_hidden
```

```python
import functools

import jax
import jax.numpy as jnp
from jax import lax
from jax.experimental import pallas as pl
from jax.experimental.pallas import tpu as pltpu
from jax.sharding import PartitionSpec as P

F32 = jnp.float32
BF16 = jnp.bfloat16
SUB = 8


def iota(shape, axis):
    return lax.broadcasted_iota(jnp.int32, shape, axis)


def pack_kernel(blocks, routes_ref, gates_ref, rows_ref, send_ref, rank_ref, mass_ref):
    tokens, width = rows_ref.shape
    out_rows = send_ref.shape[0]
    experts = out_rows // SUB
    part = width // blocks
    routes = routes_ref[...]
    gates = gates_ref[...].astype(F32)
    onehot = (iota((experts, tokens), 0) == routes).astype(F32)
    earlier = (iota((tokens, tokens), 0) < iota((tokens, tokens), 1)).astype(BF16)
    before = jnp.dot(onehot.astype(BF16), earlier, preferred_element_type=F32)
    rank = jnp.sum(before * onehot, axis=0, keepdims=True).astype(jnp.int32)
    rank_ref[...] = rank
    mass = jnp.sum(onehot * gates, axis=1, keepdims=True)
    lane = iota((SUB, mass_ref.shape[1]), 1)
    total = jnp.zeros(mass_ref.shape, F32)
    for half in range(experts // SUB):
        total += jnp.where(lane == 2 + half, mass[half * SUB : (half + 1) * SUB], 0.0)
    mass_ref[...] = total
    row = iota((out_rows, tokens), 0)
    first = jnp.where(rank < SUB, routes * SUB + rank, -1)
    pick = jnp.where(row == first, gates, 0.0).astype(BF16)
    send_ref[:, :width] = jnp.dot(pick, rows_ref[...], preferred_element_type=F32).astype(BF16)
    late = jnp.where(rank >= SUB, routes * SUB + (rank - SUB) * blocks, -out_rows)
    tail = jnp.zeros((out_rows, part), F32)
    for b in range(blocks):
        pick = jnp.where(row == late + b, gates, 0.0).astype(BF16)
        tail += jnp.dot(pick, rows_ref[:, b * part : (b + 1) * part], preferred_element_type=F32)
    send_ref[:, width:] = tail.astype(BF16)


def hidden_kernel(blocks, slots, recv_ref, w_ref, hid_ref, mass_ref, dhid_ref, ret_ref, x_ref, score_ref):
    rows = recv_ref.shape[0]
    width = x_ref.shape[1]
    part = width // blocks
    groups = rows // SUB
    late = slots - SUB
    step = pl.program_id(0)

    @pl.when(step == 0)
    def _():
        x_ref[:rows, :] = recv_ref[:, :width]
        block = iota((rows, part), 0) % blocks
        tail = recv_ref[:, width:]
        for b in range(blocks):
            x_ref[rows:, b * part : (b + 1) * part] = jnp.where(block == b, tail, jnp.zeros_like(tail))
        score_ref[...] = jnp.zeros_like(score_ref)

    proj = lax.dot_general(
        x_ref[...], w_ref[...], (((1,), (1,)), ((), ())), preferred_element_type=F32
    )
    units = proj.shape[1]
    r = iota((rows, slots * groups), 0)
    q = iota((rows, slots * groups), 1)
    hid = hid_ref[...]
    pick_main = ((q // groups == r % SUB) & (q % groups == r // SUB)).astype(BF16)
    pick_late = ((q // groups == SUB + (r % SUB) // blocks) & (q % groups == r // SUB)).astype(BF16)
    main_hid = jnp.dot(pick_main, hid, preferred_element_type=F32)
    late_hid = jnp.dot(pick_late, hid, preferred_element_type=F32)
    main = jnp.sum(main_hid * proj[:rows], axis=1, keepdims=True)
    rest = jnp.sum(late_hid * proj[rows:], axis=1, keepdims=True)
    lane = iota(score_ref.shape, 1)
    score_ref[...] += jnp.where(lane == 0, main, 0.0) + jnp.where(lane == 1, rest, 0.0)
    late_proj = jnp.sum(proj[rows:].reshape(groups * late, blocks, units), axis=1)
    o = iota((slots * groups, rows), 0)
    i = iota((slots * groups, rows), 1)
    put_main = ((o // groups == i % SUB) & (o % groups == i // SUB)).astype(BF16)
    o = iota((slots * groups, groups * late), 0)
    i = iota((slots * groups, groups * late), 1)
    put_late = ((o // groups == SUB + i % late) & (o % groups == i // late)).astype(BF16)
    out = jnp.dot(put_main, proj[:rows].astype(BF16), preferred_element_type=F32)
    out += jnp.dot(put_late, late_proj.astype(BF16), preferred_element_type=F32)
    dhid_ref[...] = out.astype(BF16)

    @pl.when(step == pl.num_programs(0) - 1)
    def _():
        mass = jnp.broadcast_to(mass_ref[...][None], (groups, SUB, mass_ref.shape[1]))
        ret_ref[...] = score_ref[...] + mass.reshape(score_ref.shape)


def probs_kernel(blocks, scale, coef_ref, routes_ref, gates_ref, rank_ref, back_ref, out_ref):
    experts, tokens = out_ref.shape
    rows = back_ref.shape[0]
    routes = routes_ref[...]
    rank = rank_ref[...]
    gates = gates_ref[...].astype(F32)
    back = back_ref[...]
    row = iota((rows, tokens), 0)
    first = jnp.where(rank < SUB, routes * SUB + rank, -1)
    late = jnp.where(rank >= SUB, routes * (SUB // blocks) + (rank - SUB), -1)
    hits = jnp.where(row == first, back[:, 0:1], 0.0)
    hits += jnp.where(row // blocks == late, back[:, 1:2], 0.0)
    score = jnp.sum(hits, axis=0, keepdims=True) / gates
    mass = jnp.sum(back.reshape(rows // SUB, SUB, back.shape[1]), axis=0)
    coef = coef_ref[0, 0] * scale
    for half in range(experts // SUB):
        expert = iota((SUB, tokens), 0) + half * SUB
        load = mass[:, 2 + half : 3 + half] * coef
        out_ref[half * SUB : (half + 1) * SUB, :] = load + jnp.where(expert == routes, score, 0.0)


def on_device(d_out, routes, gates, slot_hidden, w_down, balance_coef):
    tokens, width = d_out.shape
    groups = lax.axis_size("expert")
    dp = lax.axis_size("dp")
    experts = groups * w_down.shape[0]
    slots, units = slot_hidden.shape[3:]
    blocks = SUB // (slots - SUB)
    part = width // blocks
    out_rows = experts * SUB
    routes_row = routes.reshape(1, tokens)
    gates_row = gates.reshape(1, tokens)
    vmem = pltpu.CompilerParams(vmem_limit_bytes=48 * 1024 * 1024)

    send, rank, mass = pl.pallas_call(
        functools.partial(pack_kernel, blocks),
        out_shape=(
            jax.ShapeDtypeStruct((out_rows, width + part), BF16),
            jax.ShapeDtypeStruct((1, tokens), jnp.int32),
            jax.ShapeDtypeStruct((SUB, 128), F32),
        ),
        compiler_params=vmem,
        name="pack",
    )(routes_row, gates_row, d_out)
    recv = lax.all_to_all(send, "expert", split_axis=0, concat_axis=0, tiled=True)
    shift = 1
    while shift < dp:
        mass = mass + lax.ppermute(mass, "dp", [(s, s ^ shift) for s in range(dp)])
        shift *= 2
    hid = jnp.transpose(slot_hidden, (0, 2, 3, 1, 4)).reshape(slots * groups, units)
    chunk = 256
    d_hid, ret = pl.pallas_call(
        functools.partial(hidden_kernel, blocks, slots),
        grid=(units // chunk,),
        in_specs=[
            pl.BlockSpec((out_rows, width + part), lambda i: (0, 0)),
            pl.BlockSpec((chunk, width), lambda i: (i, 0)),
            pl.BlockSpec((slots * groups, chunk), lambda i: (0, i)),
            pl.BlockSpec((SUB, 128), lambda i: (0, 0)),
        ],
        out_specs=(
            pl.BlockSpec((slots * groups, chunk), lambda i: (0, i)),
            pl.BlockSpec((out_rows, 128), lambda i: (0, 0)),
        ),
        out_shape=(
            jax.ShapeDtypeStruct((slots * groups, units), BF16),
            jax.ShapeDtypeStruct((out_rows, 128), F32),
        ),
        scratch_shapes=[
            pltpu.VMEM((2 * out_rows, width), BF16),
            pltpu.VMEM((out_rows, 128), F32),
        ],
        compiler_params=vmem,
        name="hidden",
    )(recv, w_down.reshape(w_down.shape[1:]), hid, mass)
    back = lax.all_to_all(ret, "expert", split_axis=0, concat_axis=0, tiled=True)
    scale = experts / (routes.shape[1] * tokens * dp * groups)
    probs = pl.pallas_call(
        functools.partial(probs_kernel, blocks, scale),
        in_specs=[pl.BlockSpec(memory_space=pltpu.SMEM)] + [pl.BlockSpec(memory_space=pltpu.VMEM)] * 4,
        out_shape=jax.ShapeDtypeStruct((experts, tokens), F32),
        compiler_params=vmem,
        name="probs",
    )(balance_coef.reshape(1, 1), routes_row, gates_row, rank, back)
    d_hidden = jnp.transpose(d_hid.reshape(1, 1, slots, groups, units), (0, 3, 1, 2, 4))
    return (probs.T, d_hidden)


def solution(mesh):
    return jax.shard_map(
        on_device,
        mesh=mesh,
        in_specs=(
            P(("dp", "expert"), None),
            P(("dp", "expert"), None),
            P(("dp", "expert"), None),
            P("dp", None, "expert", None, None),
            P("expert", None, None),
            P(),
        ),
        out_specs=(P(("dp", "expert"), None), P("dp", None, "expert", None, None)),
        check_vma=False,
    )
```

```python
import functools

import jax
import jax.numpy as jnp
from jax import lax
from jax.experimental import pallas as pl
from jax.experimental.pallas import tpu as pltpu
from jax.sharding import PartitionSpec as P

F32 = jnp.float32
BF16 = jnp.bfloat16
SUB = 8


def iota(shape, axis):
    return lax.broadcasted_iota(jnp.int32, shape, axis)


def pack_kernel(
    blocks, routes_any, gates_any, rows_any, send_ref, rank_ref, mass_ref, routes_ref, gates_ref, rows_ref, sems
):
    copies = [
        pltpu.make_async_copy(routes_any, routes_ref, sems.at[0]),
        pltpu.make_async_copy(gates_any, gates_ref, sems.at[1]),
        pltpu.make_async_copy(rows_any, rows_ref, sems.at[2]),
    ]
    for copy in copies:
        copy.start()
    tokens, width = rows_ref.shape
    out_rows = send_ref.shape[0]
    experts = out_rows // SUB
    part = width // blocks
    copies[0].wait()
    copies[1].wait()
    routes = routes_ref[...]
    gates = gates_ref[...].astype(F32)
    onehot = (iota((experts, tokens), 0) == routes).astype(F32)
    earlier = (iota((tokens, tokens), 0) < iota((tokens, tokens), 1)).astype(BF16)
    before = jnp.dot(onehot.astype(BF16), earlier, preferred_element_type=F32)
    rank = jnp.sum(before * onehot, axis=0, keepdims=True).astype(jnp.int32)
    rank_ref[...] = rank
    mass = jnp.sum(onehot * gates, axis=1, keepdims=True)
    lane = iota((SUB, mass_ref.shape[1]), 1)
    total = jnp.zeros(mass_ref.shape, F32)
    for half in range(experts // SUB):
        total += jnp.where(lane == 2 + half, mass[half * SUB : (half + 1) * SUB], 0.0)
    mass_ref[...] = total
    row = iota((out_rows, tokens), 0)
    first = jnp.where(rank < SUB, routes * SUB + rank, -1)
    pick = jnp.where(row == first, gates, 0.0).astype(BF16)
    late = jnp.where(rank >= SUB, routes * SUB + (rank - SUB) * blocks, -out_rows)
    picks = [jnp.where(row == late + b, gates, 0.0).astype(BF16) for b in range(blocks)]
    copies[2].wait()
    send_ref[:, :width] = jnp.dot(pick, rows_ref[...], preferred_element_type=F32).astype(BF16)
    tail = jnp.zeros((out_rows, part), F32)
    for b in range(blocks):
        tail += jnp.dot(picks[b], rows_ref[:, b * part : (b + 1) * part], preferred_element_type=F32)
    send_ref[:, width:] = tail.astype(BF16)


def slot_of(blocks, groups, rows, columns, late):
    r = iota((rows, columns), 0)
    q = iota((rows, columns), 1)
    slot = SUB + (r % SUB) // blocks if late else r % SUB
    return (q // groups == slot) & (q % groups == r // SUB)


def expert_kernel(blocks, slots, hid_ref, w_ref, y_ref, pick_ref, tail_ref):
    rows = y_ref.shape[0]
    groups = rows // SUB
    width = y_ref.shape[1] - w_ref.shape[1]
    part = width // blocks
    step = pl.program_id(0)

    @pl.when(step == 0)
    def _():
        shape = (blocks, groups, rows, slots * groups)
        main = slot_of(*shape, False).astype(BF16)
        late = slot_of(*shape, True).astype(BF16)
        pick_ref[:rows, :] = jnp.dot(main, hid_ref[...], preferred_element_type=F32).astype(BF16)
        pick_ref[rows:, :] = jnp.dot(late, hid_ref[...], preferred_element_type=F32).astype(BF16)

    y = jnp.dot(pick_ref[...], w_ref[...], preferred_element_type=F32).astype(BF16)
    y_ref[:, pl.ds(pl.multiple_of(step * part, part), part)] = y[:rows]
    block = iota((rows, part), 0) % blocks
    tail_ref[...] = jnp.where(block == step, y[rows:], tail_ref[...])

    @pl.when(step == blocks - 1)
    def _():
        y_ref[:, width:] = tail_ref[...]


def score_kernel(width, recv_ref, y_ref, mass_ref, ret_ref):
    rows = recv_ref.shape[0]
    groups = rows // SUB
    main = jnp.zeros((rows, 128), F32)
    rest = jnp.zeros((rows, 128), F32)
    for lane in range(0, recv_ref.shape[1], 128):
        cut = slice(lane, lane + 128)
        term = recv_ref[:, cut].astype(F32) * y_ref[:, cut].astype(F32)
        if lane < width:
            main += term
        else:
            rest += term
    lane = iota(ret_ref.shape, 1)
    ret = jnp.where(lane == 0, jnp.sum(main, axis=1, keepdims=True), 0.0)
    ret += jnp.where(lane == 1, jnp.sum(rest, axis=1, keepdims=True), 0.0)
    mass = jnp.broadcast_to(mass_ref[...][None], (groups, SUB, mass_ref.shape[1]))
    ret_ref[...] = ret + mass.reshape(ret_ref.shape)


def hidden_kernel(blocks, slots, recv_ref, w_ref, after_any, dhid_ref, x_ref):
    del after_any
    rows = recv_ref.shape[0]
    width = x_ref.shape[1]
    part = width // blocks
    groups = rows // SUB
    late = slots - SUB

    @pl.when(pl.program_id(0) == 0)
    def _():
        x_ref[:rows, :] = recv_ref[:, :width]
        block = iota((rows, part), 0) % blocks
        tail = recv_ref[:, width:]
        for b in range(blocks):
            x_ref[rows:, b * part : (b + 1) * part] = jnp.where(block == b, tail, jnp.zeros_like(tail))

    proj = lax.dot_general(
        x_ref[...], w_ref[...], (((1,), (1,)), ((), ())), preferred_element_type=F32
    )
    units = proj.shape[1]
    late_proj = jnp.sum(proj[rows:].reshape(groups * late, blocks, units), axis=1)
    o = iota((slots * groups, rows), 0)
    i = iota((slots * groups, rows), 1)
    put_main = ((o // groups == i % SUB) & (o % groups == i // SUB)).astype(BF16)
    o = iota((slots * groups, groups * late), 0)
    i = iota((slots * groups, groups * late), 1)
    put_late = ((o // groups == SUB + i % late) & (o % groups == i // late)).astype(BF16)
    out = jnp.dot(put_main, proj[:rows].astype(BF16), preferred_element_type=F32)
    out += jnp.dot(put_late, late_proj.astype(BF16), preferred_element_type=F32)
    dhid_ref[...] = out.astype(BF16)


def probs_kernel(blocks, scale, coef_ref, routes_ref, gates_ref, rank_ref, back_ref, out_ref):
    experts, tokens = out_ref.shape
    rows = back_ref.shape[0]
    routes = routes_ref[...]
    rank = rank_ref[...]
    gates = gates_ref[...].astype(F32)
    back = back_ref[...]
    row = iota((rows, tokens), 0)
    first = jnp.where(rank < SUB, routes * SUB + rank, -1)
    late = jnp.where(rank >= SUB, routes * (SUB // blocks) + (rank - SUB), -1)
    hits = jnp.where(row == first, back[:, 0:1], 0.0)
    hits += jnp.where(row // blocks == late, back[:, 1:2], 0.0)
    score = jnp.sum(hits, axis=0, keepdims=True) / gates
    mass = jnp.sum(back.reshape(rows // SUB, SUB, back.shape[1]), axis=0)
    coef = coef_ref[0, 0] * scale
    for half in range(experts // SUB):
        expert = iota((SUB, tokens), 0) + half * SUB
        load = mass[:, 2 + half : 3 + half] * coef
        out_ref[half * SUB : (half + 1) * SUB, :] = load + jnp.where(expert == routes, score, 0.0)


def on_device(d_out, routes, gates, slot_hidden, w_down, balance_coef):
    tokens, width = d_out.shape
    groups = lax.axis_size("expert")
    dp = lax.axis_size("dp")
    experts = groups * w_down.shape[0]
    slots, units = slot_hidden.shape[3:]
    blocks = SUB // (slots - SUB)
    part = width // blocks
    out_rows = experts * SUB
    routes_row = routes.reshape(1, tokens)
    gates_row = gates.reshape(1, tokens)
    vmem = pltpu.CompilerParams(vmem_limit_bytes=32 * 1024 * 1024)
    anywhere = pl.BlockSpec(memory_space=pl.ANY)

    send, rank, mass = pl.pallas_call(
        functools.partial(pack_kernel, blocks),
        in_specs=[anywhere] * 3,
        out_shape=(
            jax.ShapeDtypeStruct((out_rows, width + part), BF16),
            jax.ShapeDtypeStruct((1, tokens), jnp.int32),
            jax.ShapeDtypeStruct((SUB, 128), F32),
        ),
        scratch_shapes=[
            pltpu.VMEM((1, tokens), jnp.int32),
            pltpu.VMEM((1, tokens), BF16),
            pltpu.VMEM((tokens, width), BF16),
            pltpu.SemaphoreType.DMA((3,)),
        ],
        compiler_params=pltpu.CompilerParams(vmem_limit_bytes=62 * 1024 * 1024),
        name="pack",
    )(routes_row, gates_row, d_out)
    recv = lax.all_to_all(send, "expert", split_axis=0, concat_axis=0, tiled=True)

    shift = 1
    while shift < dp:
        radix = min(4, dp // shift)
        mass = mass + sum(
            lax.ppermute(mass, "dp", [(s, s ^ (shift * k)) for s in range(dp)]) for k in range(1, radix)
        )
        shift *= radix

    hid = jnp.transpose(slot_hidden, (0, 2, 3, 1, 4)).reshape(slots * groups, units)
    weight = w_down.reshape(w_down.shape[1:])
    work = 2 * 2 * out_rows * width * units
    moved = 2 * units * width
    y_out = pl.pallas_call(
        functools.partial(expert_kernel, blocks, slots),
        grid=(blocks,),
        in_specs=[
            pl.BlockSpec((slots * groups, units), lambda i: (0, 0)),
            pl.BlockSpec((units, part), lambda i: (0, i)),
        ],
        out_specs=pl.BlockSpec((out_rows, width + part), lambda i: (0, 0)),
        out_shape=jax.ShapeDtypeStruct((out_rows, width + part), BF16),
        scratch_shapes=[
            pltpu.VMEM((2 * out_rows, units), BF16),
            pltpu.VMEM((out_rows, part), BF16),
        ],
        compiler_params=vmem,
        cost_estimate=pl.CostEstimate(flops=work, bytes_accessed=moved, transcendentals=0),
        name="expert",
    )(hid, weight)
    ret = pl.pallas_call(
        functools.partial(score_kernel, width),
        out_shape=jax.ShapeDtypeStruct((out_rows, 128), F32),
        compiler_params=vmem,
        name="score",
    )(recv, y_out, mass)
    back = lax.all_to_all(ret, "expert", split_axis=0, concat_axis=0, tiled=True)
    chunk = 256
    d_hid = pl.pallas_call(
        functools.partial(hidden_kernel, blocks, slots),
        grid=(units // chunk,),
        in_specs=[
            pl.BlockSpec((out_rows, width + part), lambda i: (0, 0)),
            pl.BlockSpec((chunk, width), lambda i: (i, 0)),
            anywhere,
        ],
        out_specs=pl.BlockSpec((slots * groups, chunk), lambda i: (0, i)),
        out_shape=jax.ShapeDtypeStruct((slots * groups, units), BF16),
        scratch_shapes=[pltpu.VMEM((2 * out_rows, width), BF16)],
        compiler_params=vmem,
        cost_estimate=pl.CostEstimate(flops=work, bytes_accessed=moved, transcendentals=0),
        name="hidden",
    )(recv, weight, ret)
    scale = experts / (routes.shape[1] * tokens * dp * groups)
    probs = pl.pallas_call(
        functools.partial(probs_kernel, blocks, scale),
        in_specs=[pl.BlockSpec(memory_space=pltpu.SMEM)] + [pl.BlockSpec(memory_space=pltpu.VMEM)] * 4,
        out_shape=jax.ShapeDtypeStruct((experts, tokens), F32),
        compiler_params=vmem,
        name="probs",
    )(balance_coef.reshape(1, 1), routes_row, gates_row, rank, back)
    d_hidden = jnp.transpose(d_hid.reshape(1, 1, slots, groups, units), (0, 3, 1, 2, 4))
    return (probs.T, d_hidden)


def solution(mesh):
    return jax.shard_map(
        on_device,
        mesh=mesh,
        in_specs=(
            P(("dp", "expert"), None),
            P(("dp", "expert"), None),
            P(("dp", "expert"), None),
            P("dp", None, "expert", None, None),
            P("expert", None, None),
            P(),
        ),
        out_specs=(P(("dp", "expert"), None), P("dp", None, "expert", None, None)),
        check_vma=False,
    )
```

```python
import functools

import jax
import jax.numpy as jnp
from jax import lax
from jax.experimental import pallas as pl
from jax.experimental.pallas import tpu as pltpu
from jax.sharding import PartitionSpec as P

F32 = jnp.float32
BF16 = jnp.bfloat16
SUB = 8


RING = 8


def iota(shape, axis):
    return lax.broadcasted_iota(jnp.int32, shape, axis)


def pack_kernel(
    blocks, routes_any, gates_any, rows_any, send_ref, rank_ref, mass_ref, routes_ref, gates_ref, rows_ref, sems
):
    copies = [
        pltpu.make_async_copy(routes_any, routes_ref, sems.at[0]),
        pltpu.make_async_copy(gates_any, gates_ref, sems.at[1]),
        pltpu.make_async_copy(rows_any, rows_ref, sems.at[2]),
    ]
    for copy in copies:
        copy.start()
    tokens, width = rows_ref.shape
    out_rows = send_ref.shape[0]
    experts = out_rows // SUB
    part = width // blocks
    copies[0].wait()
    copies[1].wait()
    routes = routes_ref[...]
    gates = gates_ref[...].astype(F32)
    onehot = (iota((experts, tokens), 0) == routes).astype(F32)
    earlier = (iota((tokens, tokens), 0) < iota((tokens, tokens), 1)).astype(BF16)
    before = jnp.dot(onehot.astype(BF16), earlier, preferred_element_type=F32)
    rank = jnp.sum(before * onehot, axis=0, keepdims=True).astype(jnp.int32)
    rank_ref[...] = rank
    mass = jnp.sum(onehot * gates, axis=1, keepdims=True)
    lane = iota((SUB, mass_ref.shape[1]), 1)
    total = jnp.zeros(mass_ref.shape, F32)
    for half in range(experts // SUB):
        total += jnp.where(lane == 2 + half, mass[half * SUB : (half + 1) * SUB], 0.0)
    mass_ref[...] = total
    row = iota((out_rows, tokens), 0)
    first = jnp.where(rank < SUB, routes * SUB + rank, -1)
    pick = jnp.where(row == first, gates, 0.0).astype(BF16)
    late = jnp.where(rank >= SUB, routes * SUB + (rank - SUB) * blocks, -out_rows)
    picks = [jnp.where(row == late + b, gates, 0.0).astype(BF16) for b in range(blocks)]
    copies[2].wait()
    send_ref[:, :width] = jnp.dot(pick, rows_ref[...], preferred_element_type=F32).astype(BF16)
    tail = jnp.zeros((out_rows, part), F32)
    for b in range(blocks):
        tail += jnp.dot(picks[b], rows_ref[:, b * part : (b + 1) * part], preferred_element_type=F32)
    send_ref[:, width:] = tail.astype(BF16)


def slot_of(blocks, groups, rows, columns, late):
    r = iota((rows, columns), 0)
    q = iota((rows, columns), 1)
    slot = SUB + (r % SUB) // blocks if late else r % SUB
    return (q // groups == slot) & (q % groups == r // SUB)


def expert_kernel(blocks, slots, hid_ref, w_ref, y_ref, pick_ref, tail_ref):
    rows = y_ref.shape[0]
    groups = rows // SUB
    width = y_ref.shape[1] - w_ref.shape[1]
    part = width // blocks
    step = pl.program_id(0)

    @pl.when(step == 0)
    def _():
        shape = (blocks, groups, rows, slots * groups)
        main = slot_of(*shape, False).astype(BF16)
        late = slot_of(*shape, True).astype(BF16)
        pick_ref[:rows, :] = jnp.dot(main, hid_ref[...], preferred_element_type=F32).astype(BF16)
        pick_ref[rows:, :] = jnp.dot(late, hid_ref[...], preferred_element_type=F32).astype(BF16)

    y = jnp.dot(pick_ref[...], w_ref[...], preferred_element_type=F32).astype(BF16)
    y_ref[:, pl.ds(pl.multiple_of(step * part, part), part)] = y[:rows]
    block = iota((rows, part), 0) % blocks
    tail_ref[...] = jnp.where(block == step, y[rows:], tail_ref[...])

    @pl.when(step == blocks - 1)
    def _():
        y_ref[:, width:] = tail_ref[...]


def score_kernel(width, recv_ref, y_ref, mass_ref, ret_ref):
    rows = recv_ref.shape[0]
    groups = rows // SUB
    main = jnp.zeros((rows, 128), F32)
    rest = jnp.zeros((rows, 128), F32)
    for lane in range(0, recv_ref.shape[1], 128):
        cut = slice(lane, lane + 128)
        term = recv_ref[:, cut].astype(F32) * y_ref[:, cut].astype(F32)
        if lane < width:
            main += term
        else:
            rest += term
    lane = iota(ret_ref.shape, 1)
    ret = jnp.where(lane == 0, jnp.sum(main, axis=1, keepdims=True), 0.0)
    ret += jnp.where(lane == 1, jnp.sum(rest, axis=1, keepdims=True), 0.0)
    mass = jnp.broadcast_to(mass_ref[...][None], (groups, SUB, mass_ref.shape[1]))
    ret_ref[...] = ret + mass.reshape(ret_ref.shape)


def hidden_kernel(blocks, slots, recv_ref, w_ref, after_any, dhid_ref, x_ref):
    del after_any
    rows = recv_ref.shape[0]
    width = x_ref.shape[1]
    part = width // blocks
    groups = rows // SUB
    late = slots - SUB

    @pl.when(pl.program_id(0) == 0)
    def _():
        x_ref[:rows, :] = recv_ref[:, :width]
        block = iota((rows, part), 0) % blocks
        tail = recv_ref[:, width:]
        for b in range(blocks):
            x_ref[rows:, b * part : (b + 1) * part] = jnp.where(block == b, tail, jnp.zeros_like(tail))

    proj = lax.dot_general(
        x_ref[...], w_ref[...], (((1,), (1,)), ((), ())), preferred_element_type=F32
    )
    units = proj.shape[1]
    late_proj = jnp.sum(proj[rows:].reshape(groups * late, blocks, units), axis=1)
    o = iota((slots * groups, rows), 0)
    i = iota((slots * groups, rows), 1)
    put_main = ((o // groups == i % SUB) & (o % groups == i // SUB)).astype(BF16)
    o = iota((slots * groups, groups * late), 0)
    i = iota((slots * groups, groups * late), 1)
    put_late = ((o // groups == SUB + i % late) & (o % groups == i // late)).astype(BF16)
    out = jnp.dot(put_main, proj[:rows].astype(BF16), preferred_element_type=F32)
    out += jnp.dot(put_late, late_proj.astype(BF16), preferred_element_type=F32)
    dhid_ref[...] = out.astype(BF16)


def probs_kernel(blocks, scale, coef_ref, routes_ref, gates_ref, rank_ref, back_ref, out_ref):
    experts, tokens = out_ref.shape
    rows = back_ref.shape[0]
    routes = routes_ref[...]
    rank = rank_ref[...]
    gates = gates_ref[...].astype(F32)
    back = back_ref[...]
    row = iota((rows, tokens), 0)
    first = jnp.where(rank < SUB, routes * SUB + rank, -1)
    late = jnp.where(rank >= SUB, routes * (SUB // blocks) + (rank - SUB), -1)
    hits = jnp.where(row == first, back[:, 0:1], 0.0)
    hits += jnp.where(row // blocks == late, back[:, 1:2], 0.0)
    score = jnp.sum(hits, axis=0, keepdims=True) / gates
    mass = jnp.sum(back.reshape(rows // SUB, SUB, back.shape[1]), axis=0)
    coef = coef_ref[0, 0] * scale
    for half in range(experts // SUB):
        expert = iota((SUB, tokens), 0) + half * SUB
        load = mass[:, 2 + half : 3 + half] * coef
        out_ref[half * SUB : (half + 1) * SUB, :] = load + jnp.where(expert == routes, score, 0.0)


def on_device(d_out, routes, gates, slot_hidden, w_down, balance_coef):
    tokens, width = d_out.shape
    groups = lax.axis_size("expert")
    dp = lax.axis_size("dp")
    experts = groups * w_down.shape[0]
    slots, units = slot_hidden.shape[3:]
    blocks = SUB // (slots - SUB)
    part = width // blocks
    out_rows = experts * SUB
    routes_row = routes.reshape(1, tokens)
    gates_row = gates.reshape(1, tokens)
    vmem = pltpu.CompilerParams(vmem_limit_bytes=32 * 1024 * 1024)
    streams = pltpu.CompilerParams(vmem_limit_bytes=50 * 1024 * 1024)
    anywhere = pl.BlockSpec(memory_space=pl.ANY)

    send, rank, mass = pl.pallas_call(
        functools.partial(pack_kernel, blocks),
        in_specs=[anywhere] * 3,
        out_shape=(
            jax.ShapeDtypeStruct((out_rows, width + part), BF16),
            jax.ShapeDtypeStruct((1, tokens), jnp.int32),
            jax.ShapeDtypeStruct((SUB, 128), F32),
        ),
        scratch_shapes=[
            pltpu.VMEM((1, tokens), jnp.int32),
            pltpu.VMEM((1, tokens), BF16),
            pltpu.VMEM((tokens, width), BF16),
            pltpu.SemaphoreType.DMA((3,)),
        ],
        compiler_params=pltpu.CompilerParams(vmem_limit_bytes=62 * 1024 * 1024),
        name="pack",
    )(routes_row, gates_row, d_out)
    recv = lax.all_to_all(send, "expert", split_axis=0, concat_axis=0, tiled=True)

    lines = [[line * RING + i for i in range(RING)] for line in range(dp // RING)]
    mass = lax.psum(mass, "dp", axis_index_groups=lines)
    mass = lax.psum(mass, "dp", axis_index_groups=[list(across) for across in zip(*lines)])

    hid = jnp.transpose(slot_hidden, (0, 2, 3, 1, 4)).reshape(slots * groups, units)
    weight = w_down.reshape(w_down.shape[1:])
    work = 2 * 2 * out_rows * width * units
    moved = 2 * units * width
    y_out = pl.pallas_call(
        functools.partial(expert_kernel, blocks, slots),
        grid=(blocks,),
        in_specs=[
            pl.BlockSpec((slots * groups, units), lambda i: (0, 0)),
            pl.BlockSpec((units, part), lambda i: (0, i)),
        ],
        out_specs=pl.BlockSpec((out_rows, width + part), lambda i: (0, 0)),
        out_shape=jax.ShapeDtypeStruct((out_rows, width + part), BF16),
        scratch_shapes=[
            pltpu.VMEM((2 * out_rows, units), BF16),
            pltpu.VMEM((out_rows, part), BF16),
        ],
        compiler_params=streams,
        cost_estimate=pl.CostEstimate(flops=work, bytes_accessed=moved, transcendentals=0),
        name="expert",
    )(hid, weight)
    ret = pl.pallas_call(
        functools.partial(score_kernel, width),
        out_shape=jax.ShapeDtypeStruct((out_rows, 128), F32),
        compiler_params=vmem,
        name="score",
    )(recv, y_out, mass)
    back = lax.all_to_all(ret, "expert", split_axis=0, concat_axis=0, tiled=True)
    chunk = 256
    d_hid = pl.pallas_call(
        functools.partial(hidden_kernel, blocks, slots),
        grid=(units // chunk,),
        in_specs=[
            pl.BlockSpec((out_rows, width + part), lambda i: (0, 0)),
            pl.BlockSpec((chunk, width), lambda i: (i, 0)),
            anywhere,
        ],
        out_specs=pl.BlockSpec((slots * groups, chunk), lambda i: (0, i)),
        out_shape=jax.ShapeDtypeStruct((slots * groups, units), BF16),
        scratch_shapes=[pltpu.VMEM((2 * out_rows, width), BF16)],
        compiler_params=streams,
        cost_estimate=pl.CostEstimate(flops=work, bytes_accessed=moved, transcendentals=0),
        name="hidden",
    )(recv, weight, ret)
    scale = experts / (routes.shape[1] * tokens * dp * groups)
    probs = pl.pallas_call(
        functools.partial(probs_kernel, blocks, scale),
        in_specs=[pl.BlockSpec(memory_space=pltpu.SMEM)] + [pl.BlockSpec(memory_space=pltpu.VMEM)] * 4,
        out_shape=jax.ShapeDtypeStruct((experts, tokens), F32),
        compiler_params=vmem,
        name="probs",
    )(balance_coef.reshape(1, 1), routes_row, gates_row, rank, back)
    d_hidden = jnp.transpose(d_hid.reshape(1, 1, slots, groups, units), (0, 3, 1, 2, 4))
    return (probs.T, d_hidden)


def solution(mesh):
    return jax.shard_map(
        on_device,
        mesh=mesh,
        in_specs=(
            P(("dp", "expert"), None),
            P(("dp", "expert"), None),
            P(("dp", "expert"), None),
            P("dp", None, "expert", None, None),
            P("expert", None, None),
            P(),
        ),
        out_specs=(P(("dp", "expert"), None), P("dp", None, "expert", None, None)),
        check_vma=False,
    )
```

```python
import functools

import jax
import jax.numpy as jnp
from jax import lax
from jax.experimental import pallas as pl
from jax.experimental.pallas import tpu as pltpu
from jax.sharding import PartitionSpec as P

F32 = jnp.float32
BF16 = jnp.bfloat16
SUB = 8


RING = 8


def iota(shape, axis):
    return lax.broadcasted_iota(jnp.int32, shape, axis)


def interleave(tail_ref, blocks, start, late):
    tiles = tail_ref.shape[0]
    for k in range(late.shape[1] // 128):
        b, tile = divmod(start + k, tiles)
        tail_ref[tile, pl.ds(b, late.shape[0], stride=blocks), :] = late[:, k * 128 : (k + 1) * 128]


def pack_kernel(
    blocks, routes_any, gates_any, rows_any, send_ref, rank_ref, mass_ref, routes_ref, gates_ref, rows_ref, tail_ref, sems
):
    copies = [
        pltpu.make_async_copy(routes_any, routes_ref, sems.at[0]),
        pltpu.make_async_copy(gates_any, gates_ref, sems.at[1]),
        pltpu.make_async_copy(rows_any, rows_ref, sems.at[2]),
    ]
    for copy in copies:
        copy.start()
    tokens, width = rows_ref.shape
    out_rows = send_ref.shape[0]
    experts = out_rows // SUB
    part = width // blocks
    copies[0].wait()
    copies[1].wait()
    routes = routes_ref[...]
    gates = gates_ref[...].astype(F32)
    onehot = (iota((experts, tokens), 0) == routes).astype(F32)
    earlier = (iota((tokens, tokens), 0) < iota((tokens, tokens), 1)).astype(BF16)
    before = jnp.dot(onehot.astype(BF16), earlier, preferred_element_type=F32)
    rank = jnp.sum(before * onehot, axis=0, keepdims=True).astype(jnp.int32)
    rank_ref[...] = rank
    mass = jnp.sum(onehot * gates, axis=1, keepdims=True)
    lane = iota((SUB, mass_ref.shape[1]), 1)
    total = jnp.zeros(mass_ref.shape, F32)
    for half in range(experts // SUB):
        total += jnp.where(lane == 2 + half, mass[half * SUB : (half + 1) * SUB], 0.0)
    mass_ref[...] = total
    late_rows = out_rows // blocks
    row = iota((out_rows + late_rows, tokens), 0)
    late = out_rows + routes * (SUB // blocks) + (rank - SUB)
    place = jnp.where(rank < SUB, routes * SUB + rank, late)
    pick = jnp.where(row == place, gates, 0.0).astype(BF16)
    copies[2].wait()
    packed = jnp.dot(pick, rows_ref[...], preferred_element_type=F32)
    send_ref[:, :width] = packed[:out_rows].astype(BF16)
    interleave(tail_ref, blocks, 0, packed[out_rows:])
    for k in range(tail_ref.shape[0]):
        send_ref[:, width + k * 128 : width + (k + 1) * 128] = tail_ref[k].astype(BF16)


def slot_order(groups, slots, rows, axis):
    count = groups * slots
    line = (count, 1) if axis == 0 else (1, count)
    r = iota(line, axis)
    late = slots - SUB
    slot = jnp.where(r < rows, r % SUB, SUB + (r - rows) % late)
    source = jnp.where(r < rows, r // SUB, (r - rows) // late)
    return (iota((count, count), 1 - axis) == slot * groups + source).astype(BF16)


def expert_kernel(blocks, slots, hid_ref, w_any, y_ref, w_ref, tail_ref, sems):
    rows = y_ref.shape[0]
    groups = rows // SUB
    width = w_ref.shape[1]
    part = width // blocks
    half = part // 2
    cuts = [slice(at, at + half) for at in range(0, width, half)]
    copies = [
        pltpu.make_async_copy(w_any.at[:, cut], w_ref.at[:, cut], sems.at[i]) for i, cut in enumerate(cuts)
    ]
    for copy in copies:
        copy.start()
    order = slot_order(groups, slots, rows, 0)
    hid = jnp.dot(order, hid_ref[...], preferred_element_type=F32).astype(BF16)
    for i, cut in enumerate(cuts):
        copies[i].wait()
        y = jnp.dot(hid, w_ref[:, cut], preferred_element_type=F32)
        y_ref[:, cut] = y[:rows].astype(BF16)
        interleave(tail_ref, blocks, i * half // 128, y[rows:])
    for k in range(tail_ref.shape[0]):
        y_ref[:, width + k * 128 : width + (k + 1) * 128] = tail_ref[k].astype(BF16)


def score_kernel(width, recv_ref, y_ref, mass_ref, ret_ref):
    rows = recv_ref.shape[0]
    groups = rows // SUB
    main = jnp.zeros((rows, 128), F32)
    rest = jnp.zeros((rows, 128), F32)
    for lane in range(0, recv_ref.shape[1], 128):
        cut = slice(lane, lane + 128)
        term = recv_ref[:, cut].astype(F32) * y_ref[:, cut].astype(F32)
        if lane < width:
            main += term
        else:
            rest += term
    lane = iota(ret_ref.shape, 1)
    ret = jnp.where(lane == 0, jnp.sum(main, axis=1, keepdims=True), 0.0)
    ret += jnp.where(lane == 1, jnp.sum(rest, axis=1, keepdims=True), 0.0)
    mass = jnp.broadcast_to(mass_ref[...][None], (groups, SUB, mass_ref.shape[1]))
    ret_ref[...] = ret + mass.reshape(ret_ref.shape)


def hidden_kernel(blocks, slots, recv_ref, w_ref, after_any, dhid_ref, x_ref):
    del after_any
    rows = recv_ref.shape[0]
    width = x_ref.shape[1]
    part = width // blocks
    late_rows = rows // blocks

    @pl.when(pl.program_id(0) == 0)
    def _():
        x_ref[:rows, :] = recv_ref[:, :width]
        r = iota((late_rows, rows), 1)
        i = iota((late_rows, rows), 0)
        for b in range(blocks):
            take = (r == i * blocks + b).astype(BF16)
            late = jnp.dot(take, recv_ref[:, width:], preferred_element_type=F32)
            x_ref[rows:, b * part : (b + 1) * part] = late.astype(BF16)

    proj = lax.dot_general(
        x_ref[...], w_ref[...], (((1,), (1,)), ((), ())), preferred_element_type=F32
    )
    order = slot_order(rows // SUB, slots, rows, 1)
    dhid_ref[...] = jnp.dot(order, proj.astype(BF16), preferred_element_type=F32).astype(BF16)


def probs_kernel(blocks, scale, coef_ref, routes_ref, gates_ref, rank_ref, back_ref, out_ref):
    experts, tokens = out_ref.shape
    rows = back_ref.shape[0]
    routes = routes_ref[...]
    rank = rank_ref[...]
    gates = gates_ref[...].astype(F32)
    back = back_ref[...]
    row = iota((rows, tokens), 0)
    first = jnp.where(rank < SUB, routes * SUB + rank, -1)
    late = jnp.where(rank >= SUB, routes * (SUB // blocks) + (rank - SUB), -1)
    hits = jnp.where(row == first, back[:, 0:1], 0.0)
    hits += jnp.where(row // blocks == late, back[:, 1:2], 0.0)
    score = jnp.sum(hits, axis=0, keepdims=True) / gates
    mass = jnp.sum(back.reshape(rows // SUB, SUB, back.shape[1]), axis=0)
    coef = coef_ref[0, 0] * scale
    for half in range(experts // SUB):
        expert = iota((SUB, tokens), 0) + half * SUB
        load = mass[:, 2 + half : 3 + half] * coef
        out_ref[half * SUB : (half + 1) * SUB, :] = load + jnp.where(expert == routes, score, 0.0)


def on_device(d_out, routes, gates, slot_hidden, w_down, balance_coef):
    tokens, width = d_out.shape
    groups = lax.axis_size("expert")
    dp = lax.axis_size("dp")
    experts = groups * w_down.shape[0]
    slots, units = slot_hidden.shape[3:]
    blocks = SUB // (slots - SUB)
    part = width // blocks
    out_rows = experts * SUB
    routes_row = routes.reshape(1, tokens)
    gates_row = gates.reshape(1, tokens)
    vmem = pltpu.CompilerParams(vmem_limit_bytes=32 * 1024 * 1024)
    streams = pltpu.CompilerParams(vmem_limit_bytes=50 * 1024 * 1024)
    anywhere = pl.BlockSpec(memory_space=pl.ANY)
    whole = pl.BlockSpec(memory_space=pltpu.VMEM)

    send, rank, mass = pl.pallas_call(
        functools.partial(pack_kernel, blocks),
        in_specs=[anywhere] * 3,
        out_shape=(
            jax.ShapeDtypeStruct((out_rows, width + part), BF16),
            jax.ShapeDtypeStruct((1, tokens), jnp.int32),
            jax.ShapeDtypeStruct((SUB, 128), F32),
        ),
        scratch_shapes=[
            pltpu.VMEM((1, tokens), jnp.int32),
            pltpu.VMEM((1, tokens), BF16),
            pltpu.VMEM((tokens, width), BF16),
            pltpu.VMEM((part // 128, out_rows, 128), F32),
            pltpu.SemaphoreType.DMA((3,)),
        ],
        compiler_params=pltpu.CompilerParams(vmem_limit_bytes=62 * 1024 * 1024),
        name="pack",
    )(routes_row, gates_row, d_out)
    recv = lax.all_to_all(send, "expert", split_axis=0, concat_axis=0, tiled=True)

    lines = [[line * RING + i for i in range(RING)] for line in range(dp // RING)]
    mass = lax.psum(mass, "dp", axis_index_groups=lines)
    mass = lax.psum(mass, "dp", axis_index_groups=[list(across) for across in zip(*lines)])

    hid = jnp.transpose(slot_hidden, (0, 2, 3, 1, 4)).reshape(slots * groups, units)
    weight = w_down.reshape(w_down.shape[1:])
    work = 2 * slots * groups * width * units
    moved = 2 * units * width
    y_out = pl.pallas_call(
        functools.partial(expert_kernel, blocks, slots),
        in_specs=[whole, anywhere],
        out_specs=whole,
        out_shape=jax.ShapeDtypeStruct((out_rows, width + part), BF16),
        scratch_shapes=[
            pltpu.VMEM((units, width), BF16),
            pltpu.VMEM((part // 128, out_rows, 128), F32),
            pltpu.SemaphoreType.DMA((2 * blocks,)),
        ],
        compiler_params=streams,
        cost_estimate=pl.CostEstimate(flops=work, bytes_accessed=moved, transcendentals=0),
        name="expert",
    )(hid, weight)
    ret = pl.pallas_call(
        functools.partial(score_kernel, width),
        out_shape=jax.ShapeDtypeStruct((out_rows, 128), F32),
        compiler_params=vmem,
        name="score",
    )(recv, y_out, mass)
    back = lax.all_to_all(ret, "expert", split_axis=0, concat_axis=0, tiled=True)
    chunk = 256
    d_hid = pl.pallas_call(
        functools.partial(hidden_kernel, blocks, slots),
        grid=(units // chunk,),
        in_specs=[
            pl.BlockSpec((out_rows, width + part), lambda i: (0, 0)),
            pl.BlockSpec((chunk, width), lambda i: (i, 0)),
            anywhere,
        ],
        out_specs=pl.BlockSpec((slots * groups, chunk), lambda i: (0, i)),
        out_shape=jax.ShapeDtypeStruct((slots * groups, units), BF16),
        scratch_shapes=[pltpu.VMEM((slots * groups, width), BF16)],
        compiler_params=streams,
        cost_estimate=pl.CostEstimate(flops=work, bytes_accessed=moved, transcendentals=0),
        name="hidden",
    )(recv, weight, ret)
    scale = experts / (routes.shape[1] * tokens * dp * groups)
    probs = pl.pallas_call(
        functools.partial(probs_kernel, blocks, scale),
        in_specs=[pl.BlockSpec(memory_space=pltpu.SMEM)] + [whole] * 4,
        out_shape=jax.ShapeDtypeStruct((experts, tokens), F32),
        compiler_params=vmem,
        name="probs",
    )(balance_coef.reshape(1, 1), routes_row, gates_row, rank, back)
    d_hidden = jnp.transpose(d_hid.reshape(1, 1, slots, groups, units), (0, 3, 1, 2, 4))
    return (probs.T, d_hidden)


def solution(mesh):
    return jax.shard_map(
        on_device,
        mesh=mesh,
        in_specs=(
            P(("dp", "expert"), None),
            P(("dp", "expert"), None),
            P(("dp", "expert"), None),
            P("dp", None, "expert", None, None),
            P("expert", None, None),
            P(),
        ),
        out_specs=(P(("dp", "expert"), None), P("dp", None, "expert", None, None)),
        check_vma=False,
    )
```

```python
import functools

import jax
import jax.numpy as jnp
from jax import lax
from jax.experimental import pallas as pl
from jax.experimental.pallas import tpu as pltpu
from jax.sharding import PartitionSpec as P

F32 = jnp.float32
BF16 = jnp.bfloat16
SUB = 8


RING = 8


def iota(shape, axis):
    return lax.broadcasted_iota(jnp.int32, shape, axis)


def interleave(tail_ref, blocks, start, late):
    tiles = tail_ref.shape[0]
    for k in range(late.shape[1] // 128):
        b, tile = divmod(start + k, tiles)
        tail_ref[tile, pl.ds(b, late.shape[0], stride=blocks), :] = late[:, k * 128 : (k + 1) * 128]


def pack_kernel(
    blocks, routes_any, gates_any, rows_any, send_ref, rank_ref, mass_ref, routes_ref, gates_ref, rows_ref, tail_ref, sems
):
    quarters = [pl.ds(i * rows_ref.shape[0] // 4, rows_ref.shape[0] // 4) for i in range(4)]
    copies = [
        pltpu.make_async_copy(routes_any, routes_ref, sems.at[0]),
        pltpu.make_async_copy(gates_any, gates_ref, sems.at[1]),
    ] + [
        pltpu.make_async_copy(rows_any.at[rows], rows_ref.at[rows], sems.at[2 + i])
        for i, rows in enumerate(quarters)
    ]
    for copy in copies:
        copy.start()
    tokens, width = rows_ref.shape
    out_rows = send_ref.shape[0]
    experts = out_rows // SUB
    part = width // blocks
    copies[0].wait()
    copies[1].wait()
    routes = routes_ref[...]
    gates = gates_ref[...].astype(F32)
    onehot = (iota((experts, tokens), 0) == routes).astype(F32)
    earlier = (iota((tokens, tokens), 0) < iota((tokens, tokens), 1)).astype(BF16)
    before = jnp.dot(onehot.astype(BF16), earlier, preferred_element_type=F32)
    rank = jnp.sum(before * onehot, axis=0, keepdims=True).astype(jnp.int32)
    rank_ref[...] = rank
    mass = jnp.sum(onehot * gates, axis=1, keepdims=True)
    lane = iota((SUB, mass_ref.shape[1]), 1)
    total = jnp.zeros(mass_ref.shape, F32)
    for half in range(experts // SUB):
        total += jnp.where(lane == 2 + half, mass[half * SUB : (half + 1) * SUB], 0.0)
    mass_ref[...] = total
    late_rows = out_rows // blocks
    row = iota((out_rows + late_rows, tokens), 0)
    late = out_rows + routes * (SUB // blocks) + (rank - SUB)
    place = jnp.where(rank < SUB, routes * SUB + rank, late)
    pick = jnp.where(row == place, gates, 0.0).astype(BF16)
    for copy in copies[2:]:
        copy.wait()
    packed = jnp.dot(pick, rows_ref[...], preferred_element_type=F32)
    send_ref[:, :width] = packed[:out_rows].astype(BF16)
    interleave(tail_ref, blocks, 0, packed[out_rows:])
    for k in range(tail_ref.shape[0]):
        send_ref[:, width + k * 128 : width + (k + 1) * 128] = tail_ref[k].astype(BF16)


def slot_order(groups, slots, rows, axis):
    count = groups * slots
    line = (count, 1) if axis == 0 else (1, count)
    r = iota(line, axis)
    late = slots - SUB
    slot = jnp.where(r < rows, r % SUB, SUB + (r - rows) % late)
    source = jnp.where(r < rows, r // SUB, (r - rows) // late)
    return (iota((count, count), 1 - axis) == slot * groups + source).astype(BF16)


def expert_kernel(blocks, slots, hid_ref, w_any, y_ref, w_ref, tail_ref, sems):
    rows = y_ref.shape[0]
    groups = rows // SUB
    width = w_ref.shape[1]
    part = width // blocks
    half = part // 2
    cuts = [slice(at, at + half) for at in range(0, width, half)]
    copies = [
        pltpu.make_async_copy(w_any.at[:, cut], w_ref.at[:, cut], sems.at[i]) for i, cut in enumerate(cuts)
    ]
    for copy in copies:
        copy.start()
    order = slot_order(groups, slots, rows, 0)
    hid = jnp.dot(order, hid_ref[...], preferred_element_type=F32).astype(BF16)
    for i, cut in enumerate(cuts):
        copies[i].wait()
        y = jnp.dot(hid, w_ref[:, cut], preferred_element_type=F32)
        y_ref[:, cut] = y[:rows].astype(BF16)
        interleave(tail_ref, blocks, i * half // 128, y[rows:])
    for k in range(tail_ref.shape[0]):
        y_ref[:, width + k * 128 : width + (k + 1) * 128] = tail_ref[k].astype(BF16)


def score_kernel(width, recv_ref, y_ref, mass_ref, ret_ref):
    rows = recv_ref.shape[0]
    groups = rows // SUB
    main = jnp.zeros((rows, 128), F32)
    rest = jnp.zeros((rows, 128), F32)
    for lane in range(0, recv_ref.shape[1], 128):
        cut = slice(lane, lane + 128)
        term = recv_ref[:, cut].astype(F32) * y_ref[:, cut].astype(F32)
        if lane < width:
            main += term
        else:
            rest += term
    lane = iota(ret_ref.shape, 1)
    ret = jnp.where(lane == 0, jnp.sum(main, axis=1, keepdims=True), 0.0)
    ret += jnp.where(lane == 1, jnp.sum(rest, axis=1, keepdims=True), 0.0)
    mass = jnp.broadcast_to(mass_ref[...][None], (groups, SUB, mass_ref.shape[1]))
    ret_ref[...] = ret + mass.reshape(ret_ref.shape)


def hidden_kernel(blocks, slots, recv_ref, w_ref, after_any, dhid_ref, x_ref):
    del after_any
    rows = recv_ref.shape[0]
    width = x_ref.shape[1]
    part = width // blocks
    late_rows = rows // blocks

    @pl.when(pl.program_id(0) == 0)
    def _():
        x_ref[:rows, :] = recv_ref[:, :width]
        r = iota((late_rows, rows), 1)
        i = iota((late_rows, rows), 0)
        for b in range(blocks):
            take = (r == i * blocks + b).astype(BF16)
            late = jnp.dot(take, recv_ref[:, width:], preferred_element_type=F32)
            x_ref[rows:, b * part : (b + 1) * part] = late.astype(BF16)

    proj = lax.dot_general(
        x_ref[...], w_ref[...], (((1,), (1,)), ((), ())), preferred_element_type=F32
    )
    order = slot_order(rows // SUB, slots, rows, 1)
    dhid_ref[...] = jnp.dot(order, proj.astype(BF16), preferred_element_type=F32).astype(BF16)


def probs_kernel(blocks, scale, coef_ref, routes_ref, gates_ref, rank_ref, back_ref, out_ref):
    experts, tokens = out_ref.shape
    rows = back_ref.shape[0]
    routes = routes_ref[...]
    rank = rank_ref[...]
    gates = gates_ref[...].astype(F32)
    back = back_ref[...]
    row = iota((rows, tokens), 0)
    first = jnp.where(rank < SUB, routes * SUB + rank, -1)
    late = jnp.where(rank >= SUB, routes * (SUB // blocks) + (rank - SUB), -1)
    hits = jnp.where(row == first, back[:, 0:1], 0.0)
    hits += jnp.where(row // blocks == late, back[:, 1:2], 0.0)
    score = jnp.sum(hits, axis=0, keepdims=True) / gates
    mass = jnp.sum(back.reshape(rows // SUB, SUB, back.shape[1]), axis=0)
    coef = coef_ref[0, 0] * scale
    for half in range(experts // SUB):
        expert = iota((SUB, tokens), 0) + half * SUB
        load = mass[:, 2 + half : 3 + half] * coef
        out_ref[half * SUB : (half + 1) * SUB, :] = load + jnp.where(expert == routes, score, 0.0)


def on_device(d_out, routes, gates, slot_hidden, w_down, balance_coef):
    tokens, width = d_out.shape
    groups = lax.axis_size("expert")
    dp = lax.axis_size("dp")
    experts = groups * w_down.shape[0]
    slots, units = slot_hidden.shape[3:]
    blocks = SUB // (slots - SUB)
    part = width // blocks
    out_rows = experts * SUB
    routes_row = routes.reshape(1, tokens)
    gates_row = gates.reshape(1, tokens)
    vmem = pltpu.CompilerParams(vmem_limit_bytes=32 * 1024 * 1024)
    streams = pltpu.CompilerParams(vmem_limit_bytes=50 * 1024 * 1024)
    anywhere = pl.BlockSpec(memory_space=pl.ANY)
    whole = pl.BlockSpec(memory_space=pltpu.VMEM)

    send, rank, mass = pl.pallas_call(
        functools.partial(pack_kernel, blocks),
        in_specs=[anywhere] * 3,
        out_shape=(
            jax.ShapeDtypeStruct((out_rows, width + part), BF16),
            jax.ShapeDtypeStruct((1, tokens), jnp.int32),
            jax.ShapeDtypeStruct((SUB, 128), F32),
        ),
        scratch_shapes=[
            pltpu.VMEM((1, tokens), jnp.int32),
            pltpu.VMEM((1, tokens), BF16),
            pltpu.VMEM((tokens, width), BF16),
            pltpu.VMEM((part // 128, out_rows, 128), F32),
            pltpu.SemaphoreType.DMA((6,)),
        ],
        compiler_params=pltpu.CompilerParams(vmem_limit_bytes=62 * 1024 * 1024),
        name="pack",
    )(routes_row, gates_row, d_out)
    recv = lax.all_to_all(send, "expert", split_axis=0, concat_axis=0, tiled=True)

    lines = [[line * RING + i for i in range(RING)] for line in range(dp // RING)]
    mass = lax.psum(mass, "dp", axis_index_groups=lines)
    mass = lax.psum(mass, "dp", axis_index_groups=[list(across) for across in zip(*lines)])

    hid = jnp.transpose(slot_hidden, (0, 2, 3, 1, 4)).reshape(slots * groups, units)
    weight = w_down.reshape(w_down.shape[1:])
    work = 2 * slots * groups * width * units
    moved = 2 * units * width
    y_out = pl.pallas_call(
        functools.partial(expert_kernel, blocks, slots),
        in_specs=[whole, anywhere],
        out_specs=whole,
        out_shape=jax.ShapeDtypeStruct((out_rows, width + part), BF16),
        scratch_shapes=[
            pltpu.VMEM((units, width), BF16),
            pltpu.VMEM((part // 128, out_rows, 128), F32),
            pltpu.SemaphoreType.DMA((2 * blocks,)),
        ],
        compiler_params=streams,
        cost_estimate=pl.CostEstimate(flops=work, bytes_accessed=moved, transcendentals=0),
        name="expert",
    )(hid, weight)
    ret = pl.pallas_call(
        functools.partial(score_kernel, width),
        out_shape=jax.ShapeDtypeStruct((out_rows, 128), F32),
        compiler_params=vmem,
        name="score",
    )(recv, y_out, mass)
    back = lax.all_to_all(ret, "expert", split_axis=0, concat_axis=0, tiled=True)
    chunk = 256
    d_hid = pl.pallas_call(
        functools.partial(hidden_kernel, blocks, slots),
        grid=(units // chunk,),
        in_specs=[
            pl.BlockSpec((out_rows, width + part), lambda i: (0, 0)),
            pl.BlockSpec((chunk, width), lambda i: (i, 0)),
            anywhere,
        ],
        out_specs=pl.BlockSpec((slots * groups, chunk), lambda i: (0, i)),
        out_shape=jax.ShapeDtypeStruct((slots * groups, units), BF16),
        scratch_shapes=[pltpu.VMEM((slots * groups, width), BF16)],
        compiler_params=streams,
        cost_estimate=pl.CostEstimate(flops=work, bytes_accessed=moved, transcendentals=0),
        name="hidden",
    )(recv, weight, ret)
    scale = experts / (routes.shape[1] * tokens * dp * groups)
    probs = pl.pallas_call(
        functools.partial(probs_kernel, blocks, scale),
        in_specs=[pl.BlockSpec(memory_space=pltpu.SMEM)] + [whole] * 4,
        out_shape=jax.ShapeDtypeStruct((experts, tokens), F32),
        compiler_params=vmem,
        name="probs",
    )(balance_coef.reshape(1, 1), routes_row, gates_row, rank, back)
    d_hidden = jnp.transpose(d_hid.reshape(1, 1, slots, groups, units), (0, 3, 1, 2, 4))
    return (probs.T, d_hidden)


def solution(mesh):
    return jax.shard_map(
        on_device,
        mesh=mesh,
        in_specs=(
            P(("dp", "expert"), None),
            P(("dp", "expert"), None),
            P(("dp", "expert"), None),
            P("dp", None, "expert", None, None),
            P("expert", None, None),
            P(),
        ),
        out_specs=(P(("dp", "expert"), None), P("dp", None, "expert", None, None)),
        check_vma=False,
    )
```
